32 devices in a mesh: fsdp: 8 (over y, x, core), tp: 4 (over z).
Axes of the slice: x: 2, y: 2, z: 4, core: 2. Of those that a mesh axis runs over, the one named last changes fastest.
Arguments:
- inputs: bfloat16 [16, 1184, 1024], P('fsdp', 'tp'), may hold values from -6 to 6
- cotangent: bfloat16 [16, 1184, 1024], P('fsdp', 'tp'), may hold values from -6 to 6
- counts: int32 [16], P('fsdp'), may hold values from 1 to 2, as said below
- first_gain: bfloat16 [1024], P('fsdp'), may hold values from 0.099609375 to 1.8984375
- first_bias: bfloat16 [1024], P('fsdp'), may hold values from -1.75 to 1.75
- query_key_value_weight: bfloat16 [1024, 3, 1024], P('fsdp', None, 'tp'), may hold values from -0.1875 to 0.1875
- project_bias: bfloat16 [2, 1024], P(None, 'tp'), may hold values from -3 to 3
- output_weight: bfloat16 [1024, 1024], P('tp', 'fsdp'), may hold values from -2 to 2
- output_bias: bfloat16 [1024], P('fsdp'), may hold values from -1.75 to 1.75
- second_gain: bfloat16 [1024], P('fsdp'), may hold values from 0.099609375 to 1.8984375
- second_bias: bfloat16 [1024], P('fsdp'), may hold values from -1.75 to 1.75
- expand_weight: bfloat16 [1024, 4096], P('fsdp', 'tp'), may hold values from -0.1875 to 0.1875
- expand_bias: bfloat16 [4096], P('tp'), may hold values from -3 to 3
- shrink_weight: bfloat16 [4096, 1024], P('tp', 'fsdp'), may hold values from -0.09375 to 0.09375
- shrink_bias: bfloat16 [1024], P('fsdp'), may hold values from -1.75 to 1.75
Outputs:
- outputs: bfloat16 [16, 1184, 1024], P('fsdp', 'tp')
- input_grad: bfloat16 [16, 1184, 1024], P('fsdp', 'tp')
- first_gain_grad: float32 [1024], P('fsdp')
- first_bias_grad: float32 [1024], P('fsdp')
- project_weight_grad: float32 [1024, 3, 1024], P('fsdp', None, 'tp')
- project_bias_grad: float32 [2, 1024], P(None, 'tp')
- output_weight_grad: float32 [1024, 1024], P('tp', 'fsdp')
- output_bias_grad: float32 [1024], P('fsdp')
- second_gain_grad: float32 [1024], P('fsdp')
- second_bias_grad: float32 [1024], P('fsdp')
- expand_weight_grad: float32 [1024, 4096], P('fsdp', 'tp')
- expand_bias_grad: float32 [4096], P('tp')
- shrink_weight_grad: float32 [4096, 1024], P('tp', 'fsdp')
- shrink_bias_grad: float32 [1024], P('fsdp')
The draws below stay inside these ranges and needn't reach their ends.
Inputs may be any that keep to these rules, and one draw needn't show every extreme that they name: counts[m] is the number of image slots of micro-batch m that hold an image; they are its first slots. In every draw some micro-batch is full.
All inputs are finite; a program needn't handle non-finite values.
Results may differ from the reference program's by a relative error of at most 0.018.
Values may be sent and summed in bfloat16 or wider, within the bound.
A program may use at most 192 MiB of HBM per device.

```python
import jax
import jax.numpy as jnp
from jax import lax

D = 1024
HEADS = 16
HEAD_DIM = 64
FF = 4096
SEQ = 577
SEQ_PAD = 592
CAP = 2
MB = 2
N_FSDP = 8
N_TP = 4


def draw_counts(key, part):
    key = jax.random.fold_in(key, 11)
    first_key, second_key = jax.random.split(key)
    entries = N_FSDP * MB
    drawn = jax.random.randint(first_key, (entries,), 1, CAP + 1)
    chosen = jax.random.randint(second_key, (), 0, entries)
    return jnp.where(jnp.arange(entries) == chosen, CAP, drawn).astype(jnp.int32)


def strengthened(array, stream_key, source, target, shards_of, factor):
    owner, partner = [(jnp.arange(array.shape[dim]) // (array.shape[dim] // shards_of)).reshape([-1 if axis == dim else 1 for axis in range(array.ndim)]) for dim in (source, target)]
    chosen = jax.random.permutation(stream_key, shards_of)[partner]
    strong = (owner == chosen) | (owner == (partner + shards_of // 2) % shards_of)
    return jnp.where(strong, factor * array, array)


def level_of(stream_key, dims, cuts, least, largest):
    loudness, own = 1.0, jax.random.fold_in(stream_key, 6)
    for dim, blocks in cuts:
        steps = jnp.exp(jax.random.uniform(jax.random.fold_in(own, dim), (blocks,), jnp.float32, least / len(cuts), largest / len(cuts)))
        loudness = loudness * jnp.repeat(steps, dims[dim] // blocks).reshape([-1 if axis == dim else 1 for axis in range(len(dims))])
    return loudness


def bell_draw(own_key, dims, scale, limit, shards=(), kind=jnp.bfloat16):
    values = scale * jax.random.normal(own_key, dims, jnp.float32)
    if shards:
        values = values * level_of(own_key, dims, shards, -0.22, 0.18)
    return jnp.clip(values, -limit, limit).astype(kind)


def heavy_noise(own_key, shape, spread, reach, cuts, heavy, kind=jnp.bfloat16):
    values = spread * jax.random.normal(own_key, shape, jnp.float32)
    if cuts:
        values = values * level_of(own_key, shape, cuts, -0.22, 0.18)
    return jnp.clip(strengthened(values, jax.random.fold_in(own_key, 3), *heavy), -reach, reach).astype(kind)


def setup_inputs(seed: int = 0) -> dict:
    seeds = jax.random.split(jax.random.key(seed), 16)
    return {
        "inputs": bell_draw(seeds[0], (N_FSDP * MB, CAP * SEQ_PAD, D), 1.0, 6.0, ((0, 8), (1, 4))),
        "cotangent": heavy_noise(seeds[1], (N_FSDP * MB, CAP * SEQ_PAD, D), 1.0, 6.0, ((0, 8), (1, 4)), (0, 2, 8, 2.0)),
        "counts": draw_counts(jax.random.fold_in(seeds[15], 71), 0),
        "first_gain": jnp.clip(1.0 + 0.18 * jax.random.normal(seeds[3], (D,), jnp.float32), 0.099609375, 1.8984375).astype(jnp.bfloat16),
        "first_bias": bell_draw(seeds[4], (D,), 0.3, 1.75, ((0, 8),)),
        "query_key_value_weight": bell_draw(seeds[5], (D, 3, D), D ** -0.5, 0.1875, ((0, 8), (2, 4))),
        "project_bias": bell_draw(seeds[6], (2, D), 0.5, 3.0, ((1, 4),)),
        "output_weight": bell_draw(seeds[7], (D, D), (max(D // 128, 1)) ** -0.5, 2.0, ((0, 4), (1, 8))),
        "output_bias": bell_draw(seeds[8], (D,), 0.3, 1.75, ((0, 8),)),
        "second_gain": jnp.clip(1.0 + 0.18 * jax.random.normal(seeds[9], (D,), jnp.float32), 0.099609375, 1.8984375).astype(jnp.bfloat16),
        "second_bias": bell_draw(seeds[10], (D,), 0.3, 1.75, ((0, 8),)),
        "expand_weight": bell_draw(seeds[11], (D, FF), D ** -0.5, 0.1875, ((0, 8), (1, 4))),
        "expand_bias": bell_draw(seeds[12], (FF,), 0.5, 3.0, ((0, 4),)),
        "shrink_weight": bell_draw(seeds[13], (FF, D), FF ** -0.5, 0.09375, ((0, 4), (1, 8))),
        "shrink_bias": bell_draw(seeds[14], (D,), 0.3, 1.75, ((0, 8),)),
    }


@jax.custom_vjp
def low(v):
    return lax.optimization_barrier(v.astype(jnp.bfloat16)).astype(jnp.float32)

@jax.custom_vjp
def low_back(v):
    return v

def low_keep(v):
    return (low(v), None)

def low_pass(kept, grad):
    return (grad,)

def back_keep(v):
    return (v, None)

def back_low(kept, grad):
    return (low(grad),)
low.defvjp(low_keep, low_pass)
low_back.defvjp(back_keep, back_low)
highest_precision = lax.Precision.HIGHEST
epsilon = 1e-06

def normalize(values, norm_gain, norm_bias):
    average = lax.optimization_barrier(jnp.mean(values, axis=-1, keepdims=True))
    centered = values - average
    variance = lax.optimization_barrier(jnp.mean(centered * centered, axis=-1, keepdims=True))
    return centered * lax.rsqrt(variance + epsilon) * norm_gain + norm_bias

def attend_image(triple):
    queries, keys, values = triple
    scores = low_back(jnp.einsum('qhd,khd->hqk', queries, keys, precision=highest_precision) * HEAD_DIM ** (-0.5))
    keylive = jnp.arange(SEQ_PAD) < SEQ
    scores = jnp.where(keylive[None, None, :], scores, -1e+30)
    probs = jax.nn.softmax(scores, axis=-1)
    mixed = jnp.einsum('hqk,khd->qhd', low(probs), values, precision=highest_precision)
    return low(low_back(mixed))

def copies_of(rows):
    return low_back(jnp.broadcast_to(rows[None], (N_TP,) + rows.shape))

def forward(params, block, live):
    first_gain, first_bias, query_key_value_weight, project_bias, output_weight, output_bias, second_gain, second_bias, expand_weight, expand_bias, shrink_weight, shrink_bias = params
    normalized_rows = low(normalize(block, first_gain, first_bias))
    grouped_weight = query_key_value_weight.reshape(D, 3, N_TP, D // N_TP)
    projected_rows = jnp.einsum('ghxf,fogv->hxogv', copies_of(normalized_rows), grouped_weight, precision=highest_precision).reshape(CAP, SEQ_PAD, 3, D)
    queries = low(low_back(projected_rows[:, :, 0] + project_bias[0]))
    keys = low(low_back(projected_rows[:, :, 1]))
    values = low(low_back(projected_rows[:, :, 2] + project_bias[1]))
    split_shape = (CAP, SEQ_PAD, HEADS, HEAD_DIM)
    mixed = lax.map(jax.checkpoint(attend_image), (queries.reshape(split_shape), keys.reshape(split_shape), values.reshape(split_shape)))
    mixed = mixed.reshape(CAP, SEQ_PAD, D)
    attend = low_back(jnp.einsum('ipe,ed->ipd', mixed, output_weight, precision=highest_precision) + output_bias)
    middle = block + attend
    normed_two = low(normalize(middle, second_gain, second_bias))
    grouped_expand = expand_weight.reshape(D, N_TP, FF // N_TP)
    hidden = jnp.einsum('gipd,dgf->ipgf', copies_of(normed_two), grouped_expand, precision=highest_precision).reshape(CAP, SEQ_PAD, FF)
    hidden = low_back(hidden + expand_bias)
    activated = low(jax.nn.gelu(hidden, approximate=False))
    grouped_shrink = shrink_weight.reshape(N_TP, FF // N_TP, D)
    partials = low(jnp.einsum('ipgf,gfd->gipd', activated.reshape(CAP, SEQ_PAD, N_TP, FF // N_TP), grouped_shrink, precision=highest_precision))
    branch = low_back(lax.optimization_barrier(jnp.sum(partials, axis=0)) + shrink_bias)
    return (middle + branch) * live[:, :, None]

def reference(inputs, cotangent, counts, first_gain, first_bias, query_key_value_weight, project_bias, output_weight, output_bias, second_gain, second_bias, expand_weight, expand_bias, shrink_weight, shrink_bias):
    params = tuple((item.astype(jnp.float32) for item in (first_gain, first_bias, query_key_value_weight, project_bias, output_weight, output_bias, second_gain, second_bias, expand_weight, expand_bias, shrink_weight, shrink_bias)))
    blocks = inputs.astype(jnp.float32).reshape(N_FSDP * MB, CAP, SEQ_PAD, D)
    upstream = cotangent.astype(jnp.float32).reshape(N_FSDP * MB, CAP, SEQ_PAD, D)
    image_index = jnp.arange(CAP, dtype=jnp.int32)
    position = jnp.arange(SEQ_PAD, dtype=jnp.int32)
    lives = ((image_index[None, :, None] < counts[:, None, None]) & (position[None, None, :] < SEQ)).astype(jnp.float32)

    def visit(totals, pieces):
        block, seed_grad, live = pieces
        result, pullback = jax.vjp(lambda weights, rows: forward(weights, rows, live), params, block)
        weight_grads, input_rows = pullback(seed_grad)
        totals = jax.tree.map(jnp.add, totals, weight_grads)
        return (totals, (result.astype(jnp.bfloat16), input_rows.astype(jnp.bfloat16)))
    zeros = jax.tree.map(jnp.zeros_like, params)
    totals, (results, input_rows) = lax.scan(visit, zeros, (blocks, upstream, lives))
    full_shape = (N_FSDP * MB, CAP * SEQ_PAD, D)
    return (results.reshape(full_shape), input_rows.reshape(full_shape), totals[0], totals[1], totals[2], totals[3], totals[4], totals[5], totals[6], totals[7], totals[8], totals[9], totals[10], totals[11])
```

```python
import jax
import jax.numpy as jnp
import numpy as np
from jax import lax
from jax.experimental import pallas as pl
from jax.experimental.pallas import tpu as pltpu
from jax.sharding import PartitionSpec as P

HEAD_DIM = 64
SEQ = 577
SEQ_PAD = 592
CAP = 2


epsilon = 1e-06


def forward_norm(values, norm_gain, norm_bias):
    average = jnp.mean(values, axis=-1, keepdims=True)
    centered = values - average
    variance = jnp.mean(centered * centered, axis=-1, keepdims=True)
    inverse = lax.rsqrt(variance + epsilon)
    unit = centered * inverse
    return (unit * norm_gain + norm_bias, unit, inverse)


def backward_norm(upstream, unit, inverse, norm_gain):
    scaled = upstream * norm_gain
    first = jnp.mean(scaled, axis=-1, keepdims=True)
    second = jnp.mean(scaled * unit, axis=-1, keepdims=True)
    return inverse * (scaled - first - unit * second)


def gelu_slope(hidden):
    return (
        0.5 * (1.0 + lax.erf(hidden * 0.7071067811865476))
        + hidden * jnp.exp(-0.5 * hidden * hidden) * 0.3989422804014327
    )


def attention_scores(queries, keys, factor, keylive):
    scores = (
        jnp.einsum("iqhd,ikhd->ihqk", queries, keys, preferred_element_type=jnp.float32) * factor
    )
    return jnp.where(keylive, scores, -1e30)


def per_device(
    inputs,
    cotangent,
    counts,
    first_gain,
    first_bias,
    query_key_value_weight,
    project_bias,
    output_weight,
    output_bias,
    second_gain,
    second_bias,
    expand_weight,
    expand_bias,
    shrink_weight,
    shrink_bias,
):
    local_rows = inputs.shape[1]
    local_width = query_key_value_weight.shape[2]
    local_heads = local_width // HEAD_DIM
    padded = SEQ_PAD
    all_rows = CAP * padded
    factor = HEAD_DIM ** (-0.5)
    vectors = jnp.stack(
        [first_gain, first_bias, output_bias, second_gain, second_bias, shrink_bias]
    )
    row_index = lax.axis_index("tp") * local_rows + jnp.arange(local_rows, dtype=jnp.int32)
    row_image = row_index // padded
    row_valid = row_index % padded < SEQ
    keylive = (jnp.arange(padded) < SEQ)[None, None, None, :]
    split_shape = (CAP, padded, local_heads, HEAD_DIM)
    qv_bias = project_bias.astype(jnp.float32)
    up_bias = expand_bias.astype(jnp.float32)

    def visit(totals, pieces):
        block_in, block_cot, count = pieces
        fetched = (
            lax.all_gather(query_key_value_weight, "fsdp", axis=0, tiled=True),
            lax.all_gather(output_weight, "fsdp", axis=1, tiled=True),
            lax.all_gather(expand_weight, "fsdp", axis=0, tiled=True),
            lax.all_gather(shrink_weight, "fsdp", axis=1, tiled=True),
            lax.all_gather(vectors, "fsdp", axis=1, tiled=True),
        )
        projection_weight_local, w_output, w_expand, w_shrink, vector_rows = fetched
        vector_rows = vector_rows.astype(jnp.float32)
        live = ((row_image < count) & row_valid).astype(jnp.float32)[:, None]
        block = block_in.astype(jnp.float32)
        normalized_rows, unit_one, inverse_one = forward_norm(block, vector_rows[0], vector_rows[1])
        first_token_rows = lax.all_gather(
            normalized_rows.astype(jnp.bfloat16), "tp", axis=0, tiled=True
        )
        projected_rows = jnp.einsum(
            "fk,kal->fal",
            first_token_rows,
            projection_weight_local,
            preferred_element_type=jnp.float32,
        )
        queries = (projected_rows[:, 0] + qv_bias[0]).astype(jnp.bfloat16).reshape(split_shape)
        keys = projected_rows[:, 1].astype(jnp.bfloat16).reshape(split_shape)
        values = (projected_rows[:, 2] + qv_bias[1]).astype(jnp.bfloat16).reshape(split_shape)
        scores = attention_scores(queries, keys, factor, keylive)
        row_peak = jnp.max(scores, axis=-1, keepdims=True)
        expon = jnp.exp(scores - row_peak)
        row_totals = jnp.sum(expon, axis=-1, keepdims=True)
        logsum = row_peak + jnp.log(row_totals)
        probs = (expon / row_totals).astype(jnp.bfloat16)
        mixed = (
            jnp.einsum("ihqk,ikhd->iqhd", probs, values, preferred_element_type=jnp.float32)
            .astype(jnp.bfloat16)
            .reshape(all_rows, local_width)
        )
        whole_output = lax.all_gather(w_output, "tp", axis=0, tiled=True)
        own_mixed = lax.all_to_all(mixed, "tp", split_axis=0, concat_axis=1, tiled=True)
        attend = jnp.dot(own_mixed, whole_output, preferred_element_type=jnp.float32)
        middle = block + attend + vector_rows[2]
        normed_two, unit_two, inverse_two = forward_norm(middle, vector_rows[3], vector_rows[4])
        tokens_two = lax.all_gather(normed_two.astype(jnp.bfloat16), "tp", axis=0, tiled=True)
        hidden = jnp.dot(tokens_two, w_expand, preferred_element_type=jnp.float32) + up_bias
        activated = jax.nn.gelu(hidden, approximate=False).astype(jnp.bfloat16)
        partial_two = jnp.dot(activated, w_shrink, preferred_element_type=jnp.float32)
        branch = lax.psum_scatter(
            partial_two.astype(jnp.bfloat16), "tp", scatter_dimension=0, tiled=True
        ).astype(jnp.float32)
        out_rows = ((middle + branch + vector_rows[5]) * live).astype(jnp.bfloat16)
        fetched_back = (
            lax.all_gather(query_key_value_weight, "fsdp", axis=0, tiled=True),
            lax.all_gather(output_weight, "fsdp", axis=1, tiled=True),
            lax.all_gather(expand_weight, "fsdp", axis=0, tiled=True),
            lax.all_gather(shrink_weight, "fsdp", axis=1, tiled=True),
            lax.all_gather(vectors, "fsdp", axis=1, tiled=True),
        )
        projection_back_local, b_output, b_expand, b_shrink, back_rows = fetched_back
        back_rows = back_rows.astype(jnp.float32)
        seed = (block_cot.astype(jnp.float32) * live).astype(jnp.bfloat16)
        seed_float = seed.astype(jnp.float32)
        seed_all = lax.all_gather(seed, "tp", axis=0, tiled=True)
        grad_shrink = jnp.einsum(
            "rf,rd->fd", activated, seed_all, preferred_element_type=jnp.float32
        )
        grad_hidden = (
            jnp.einsum("rd,fd->rf", seed_all, b_shrink, preferred_element_type=jnp.float32)
            * gelu_slope(hidden)
        ).astype(jnp.bfloat16)
        grad_expand = jnp.einsum(
            "rd,rf->df", tokens_two, grad_hidden, preferred_element_type=jnp.float32
        )
        grad_normed_two = lax.psum_scatter(
            jnp.einsum(
                "rf,df->rd", grad_hidden, b_expand, preferred_element_type=jnp.float32
            ).astype(jnp.bfloat16),
            "tp",
            scatter_dimension=0,
            tiled=True,
        ).astype(jnp.float32)
        grad_middle = seed_float + backward_norm(
            grad_normed_two, unit_two, inverse_two, back_rows[3]
        )
        grad_attend = grad_middle.astype(jnp.bfloat16)
        attend_all = lax.all_gather(grad_attend, "tp", axis=0, tiled=True)
        grad_output = jnp.einsum("re,rd->ed", mixed, attend_all, preferred_element_type=jnp.float32)
        grad_mixed = (
            jnp.einsum("rd,ed->re", attend_all, b_output, preferred_element_type=jnp.float32)
            .astype(jnp.bfloat16)
            .reshape(split_shape)
        )
        again = attention_scores(queries, keys, factor, keylive)
        probs_back = jnp.exp(again - logsum)
        grad_probs = jnp.einsum(
            "iqhd,ikhd->ihqk", grad_mixed, values, preferred_element_type=jnp.float32
        )
        inner = jnp.sum(grad_probs * probs_back, axis=-1, keepdims=True)
        grad_scores = (probs_back * (grad_probs - inner)).astype(jnp.bfloat16)
        grad_queries = (
            jnp.einsum("ihqk,ikhd->iqhd", grad_scores, keys, preferred_element_type=jnp.float32)
            * factor
        ).astype(jnp.bfloat16)
        grad_keys = (
            jnp.einsum("ihqk,iqhd->ikhd", grad_scores, queries, preferred_element_type=jnp.float32)
            * factor
        ).astype(jnp.bfloat16)
        grad_values = jnp.einsum(
            "ihqk,iqhd->ikhd",
            probs_back.astype(jnp.bfloat16),
            grad_mixed,
            preferred_element_type=jnp.float32,
        ).astype(jnp.bfloat16)
        stacked_rows = jnp.stack(
            [
                grad_queries.reshape(all_rows, local_width),
                grad_keys.reshape(all_rows, local_width),
                grad_values.reshape(all_rows, local_width),
            ],
            axis=1,
        )
        grad_project = jnp.einsum(
            "gz,gfo->zfo", first_token_rows, stacked_rows, preferred_element_type=jnp.float32
        )
        grad_normed = lax.psum_scatter(
            jnp.einsum(
                "inj,onj->io",
                stacked_rows,
                projection_back_local,
                preferred_element_type=jnp.float32,
            ).astype(jnp.bfloat16),
            "tp",
            scatter_dimension=0,
            tiled=True,
        ).astype(jnp.float32)
        grad_rows = (
            grad_middle + backward_norm(grad_normed, unit_one, inverse_one, back_rows[0])
        ).astype(jnp.bfloat16)
        vector_grads = jnp.stack(
            [
                jnp.sum(grad_normed * unit_one, axis=0),
                jnp.sum(grad_normed, axis=0),
                jnp.sum(grad_attend.astype(jnp.float32), axis=0),
                jnp.sum(grad_normed_two * unit_two, axis=0),
                jnp.sum(grad_normed_two, axis=0),
                jnp.sum(seed_float, axis=0),
            ]
        )
        qv_grads = jnp.sum(stacked_rows[:, 0::2].astype(jnp.float32), axis=0)
        up_grads = jnp.sum(grad_hidden.astype(jnp.float32), axis=0)
        updated = (
            totals[0] + grad_project,
            totals[1] + grad_output,
            totals[2] + grad_expand,
            totals[3] + grad_shrink,
            totals[4] + vector_grads,
            totals[5] + qv_grads,
            totals[6] + up_grads,
        )
        return (updated, (out_rows, grad_rows))

    width = inputs.shape[2]
    ff_local = expand_weight.shape[1]
    zeros = (
        jnp.zeros((width, 3, local_width), jnp.float32),
        jnp.zeros((local_width, width), jnp.float32),
        jnp.zeros((width, ff_local), jnp.float32),
        jnp.zeros((ff_local, width), jnp.float32),
        jnp.zeros((6, width), jnp.float32),
        jnp.zeros((2, local_width), jnp.float32),
        jnp.zeros((ff_local,), jnp.float32),
    )
    totals, (outputs, input_grad) = lax.scan(visit, zeros, (inputs, cotangent, counts))
    summed_vectors = lax.psum(totals[4], "tp")
    shards = (
        lax.psum_scatter(
            totals[0].astype(jnp.bfloat16), "fsdp", scatter_dimension=0, tiled=True
        ).astype(jnp.float32),
        lax.psum_scatter(
            totals[1].astype(jnp.bfloat16), "fsdp", scatter_dimension=1, tiled=True
        ).astype(jnp.float32),
        lax.psum_scatter(
            totals[2].astype(jnp.bfloat16), "fsdp", scatter_dimension=0, tiled=True
        ).astype(jnp.float32),
        lax.psum_scatter(
            totals[3].astype(jnp.bfloat16), "fsdp", scatter_dimension=1, tiled=True
        ).astype(jnp.float32),
        lax.psum_scatter(
            summed_vectors.astype(jnp.bfloat16), "fsdp", scatter_dimension=1, tiled=True
        ).astype(jnp.float32),
    )
    bias_totals = lax.psum((totals[5], totals[6]), "fsdp")
    vector_shards = shards[4]
    return (
        outputs,
        input_grad,
        vector_shards[0],
        vector_shards[1],
        shards[0],
        bias_totals[0],
        shards[1],
        vector_shards[2],
        vector_shards[3],
        vector_shards[4],
        shards[2],
        bias_totals[1],
        shards[3],
        vector_shards[5],
    )


def swapped(rows, axis, bit):
    size = lax.axis_size(axis)
    return lax.ppermute(rows, axis, [(i, i ^ bit) for i in range(size)])


CORE, X, Y = ("fsdp", 1), ("fsdp", 2), ("fsdp", 4)
Z_NEAR, Z_FAR = ("tp", 1), ("tp", 2)
WAYS = ((X, Y), (Y, X))


def gather_weight(shard):
    half = shard.shape[0] // 2
    parts = []
    for which, way in enumerate(WAYS):
        part = shard[which * half : (which + 1) * half]
        for step in (Z_FAR, Z_NEAR):
            part = jnp.concatenate([part, swapped(part, *step)], axis=1)
        for step in way:
            part = jnp.concatenate([part, swapped(part, *step)], axis=0)
        parts += [part, swapped(part, *CORE)]
    return jnp.concatenate(parts, axis=0)


def exchange_sum(kept, sent, step, kind=jnp.bfloat16):
    received = swapped(sent, *step)
    return (kept.astype(jnp.float32) + received.astype(jnp.float32)).astype(kind)


def scatter_grad(grad):
    half = grad.shape[0] // 2
    parts = []
    for which, way in enumerate(WAYS):
        part = grad[which * half : (which + 1) * half]
        for step in (CORE, way[1], way[0]):
            middle = part.shape[0] // 2
            part = exchange_sum(part[:middle], part[middle:], step)
        for step, kind in ((Z_NEAR, jnp.bfloat16), (Z_FAR, jnp.float32)):
            middle = part.shape[1] // 2
            part = exchange_sum(part[:, :middle], part[:, middle:], step, kind)
        parts.append(part)
    return jnp.concatenate(parts, axis=0)


def dot(left, right, contract):
    return lax.dot_general(
        left, right, ((contract[:1], contract[1:]), ((), ())), preferred_element_type=jnp.float32
    )


def head_probs(queries, keys, mask):
    scores = dot(queries, keys, (1, 1)) * HEAD_DIM ** (-0.5) + mask
    expon = jnp.exp(scores - jnp.max(scores, axis=-1, keepdims=True))
    return expon * (1.0 / jnp.sum(expon, axis=-1, keepdims=True))


def attend_kernel(mask_ref, project_ref, mixed_ref):
    width = mixed_ref.shape[1]
    mask = mask_ref[...]
    for head in range(width // HEAD_DIM):
        span = [slice(j * width + head * HEAD_DIM, j * width + (head + 1) * HEAD_DIM) for j in range(3)]
        queries, keys, values = (project_ref[:, s] for s in span)
        probs = head_probs(queries, keys, mask).astype(jnp.bfloat16)
        mixed_ref[:, span[0]] = dot(probs, values, (1, 0)).astype(jnp.bfloat16)


def attend_back_kernel(mask_ref, project_ref, grad_ref, out_ref):
    width = grad_ref.shape[1]
    mask = mask_ref[...]
    factor = HEAD_DIM ** (-0.5)
    for head in range(width // HEAD_DIM):
        span = [slice(j * width + head * HEAD_DIM, j * width + (head + 1) * HEAD_DIM) for j in range(3)]
        queries, keys, values = (project_ref[:, s] for s in span)
        grad_mixed = grad_ref[:, span[0]]
        probs = head_probs(queries, keys, mask)
        grad_probs = dot(grad_mixed, values, (1, 1))
        inner = jnp.sum(grad_probs * probs, axis=-1, keepdims=True)
        grad_scores = (probs * (grad_probs - inner)).astype(jnp.bfloat16)
        out_ref[:, span[0]] = (dot(grad_scores, keys, (1, 0)) * factor).astype(jnp.bfloat16)
        out_ref[:, span[1]] = (dot(grad_scores, queries, (0, 0)) * factor).astype(jnp.bfloat16)
        out_ref[:, span[2]] = dot(probs.astype(jnp.bfloat16), grad_mixed, (0, 0)).astype(jnp.bfloat16)


def attention_call(kernel, mask, operands, groups, out_width, flops):
    rows = operands[0].shape[0]

    def block(width):
        return pl.BlockSpec((rows, width), lambda g: (0, g))

    return pl.pallas_call(
        kernel,
        grid=(groups,),
        in_specs=[pl.BlockSpec((1, rows), lambda g: (0, 0))]
        + [block(item.shape[1] // groups) for item in operands],
        out_specs=block(out_width // groups),
        out_shape=jax.ShapeDtypeStruct((rows, out_width), jnp.bfloat16),
        compiler_params=pltpu.CompilerParams(vmem_limit_bytes=48 * 2**20),
        cost_estimate=pl.CostEstimate(
            flops=flops, bytes_accessed=8 * rows * out_width, transcendentals=0
        ),
    )(mask, *operands)


def per_device_whole_image(
    inputs,
    cotangent,
    counts,
    first_gain,
    first_bias,
    query_key_value_weight,
    project_bias,
    output_weight,
    output_bias,
    second_gain,
    second_bias,
    expand_weight,
    expand_bias,
    shrink_weight,
    shrink_bias,
):
    bf16, f32 = jnp.bfloat16, jnp.float32
    n_tp = lax.axis_size("tp")
    place, z = lax.axis_index("fsdp"), lax.axis_index("tp")
    odd = z % 2
    local_rows, width = inputs.shape[1:]
    depth, _, local_width = query_key_value_weight.shape
    ff_local = expand_weight.shape[1]
    rows = 2 * local_rows
    half = depth // 2

    core, first, second = (np.arange(8) >> 2) & 1, (np.arange(8) >> 1) & 1, np.arange(8) & 1
    relative = np.stack([second * 2 + first * 4 + core, first * 2 + second * 4 + core])
    offset = half * np.arange(2)[:, None, None] + np.arange(half)[None, None, :]
    absolute = (
        jnp.bitwise_xor(jnp.asarray(relative, jnp.int32), place)[:, :, None] * depth + offset
    ).reshape(width)
    placed = jnp.arange(width, dtype=jnp.int32)[:, None] == absolute[None, :]
    order = placed.astype(bf16)

    w_project = gather_weight(query_key_value_weight.reshape(depth, 3 * local_width))
    w_output = gather_weight(output_weight.T)
    w_expand = gather_weight(expand_weight)
    w_shrink = gather_weight(shrink_weight.T)
    vectors = jnp.stack(
        [first_gain, first_bias, output_bias, second_gain, second_bias, shrink_bias]
    ).reshape(6, 1, depth)
    for step in (X, Y, CORE):
        vectors = jnp.concatenate([vectors, swapped(vectors, *step)], axis=1)
    vectors = vectors.reshape(6, 2, 2, 2, 2, half)
    vectors = jnp.stack(
        [vectors[:, :, :, :, 0], jnp.swapaxes(vectors[:, :, :, :, 1], 2, 3)], axis=1
    ).reshape(6, 1, width).astype(f32)
    biases = jnp.concatenate([project_bias.reshape(1, -1), expand_bias[None]], axis=1)
    for step in (Z_FAR, Z_NEAR):
        biases = jnp.concatenate([biases, swapped(biases, *step)], axis=0)
    biases = biases.astype(f32)
    zero = jnp.zeros((n_tp, local_width), f32)
    qkv_bias = jnp.stack(
        [biases[:, :local_width], zero, biases[:, local_width : 2 * local_width]], axis=1
    ).reshape(1, -1)
    up_bias = biases[:, 2 * local_width :].reshape(1, -1)

    def fetch(whole):
        own = jnp.where(odd == 0, whole[0], whole[1])
        other = jnp.where(odd == 0, whole[1], whole[0])
        taken = jnp.concatenate([own, swapped(other, *Z_NEAR)], axis=0)
        return dot(taken, order, (1, 0))

    def give_back(taken):
        taken = dot(taken, order, (1, 1)).astype(bf16)
        own, other = taken[:local_rows], swapped(taken[local_rows:], *Z_NEAR)
        return jnp.where(odd == 0, jnp.stack([own, other]), jnp.stack([other, own]))

    index = jnp.arange(rows, dtype=jnp.int32)
    position = jnp.where(odd == 1, (index + local_rows) % rows, index)
    count = jnp.where(odd == 0, counts[0], counts[1])
    live = ((position < SEQ) & (z // 2 < count)).astype(f32)[:, None]
    mask = jnp.where(position < SEQ, 0.0, -1e30).astype(f32)[None]

    block = fetch(inputs)
    seed_float = fetch(cotangent) * live
    seed = seed_float.astype(bf16)

    normed_one, unit_one, inverse_one = forward_norm(block, vectors[0], vectors[1])
    normed_one = normed_one.astype(bf16)
    project = (dot(normed_one, w_project, (1, 0)) + qkv_bias).astype(bf16)
    pair_flops = 2 * rows * rows * width
    mixed = attention_call(attend_kernel, mask, [project], n_tp, width, 2 * pair_flops)
    middle = block + dot(mixed, w_output, (1, 1)) + vectors[2]
    normed_two, unit_two, inverse_two = forward_norm(middle, vectors[3], vectors[4])
    normed_two = normed_two.astype(bf16)
    hidden = dot(normed_two, w_expand, (1, 0)) + up_bias
    activated = jax.nn.gelu(hidden, approximate=False).astype(bf16)
    branch = dot(activated, w_shrink, (1, 1))
    outputs = give_back(((middle + branch + vectors[5]) * live).astype(bf16))

    grad_shrink = scatter_grad(dot(seed, activated, (0, 0)).astype(bf16)).T
    grad_hidden = (dot(seed, w_shrink, (1, 0)) * gelu_slope(hidden)).astype(bf16)
    grad_expand = scatter_grad(dot(normed_two, grad_hidden, (0, 0)).astype(bf16))
    grad_normed_two = dot(grad_hidden, w_expand, (1, 1))
    grad_middle = seed_float + backward_norm(grad_normed_two, unit_two, inverse_two, vectors[3])
    grad_attend = grad_middle.astype(bf16)
    grad_output = scatter_grad(dot(grad_attend, mixed, (0, 0)).astype(bf16)).T
    grad_mixed = dot(grad_attend, w_output, (1, 0)).astype(bf16)
    grad_parts = attention_call(
        attend_back_kernel, mask, [project, grad_mixed], n_tp, 3 * width, 5 * pair_flops
    )
    grad_project = scatter_grad(dot(normed_one, grad_parts, (0, 0)).astype(bf16))
    grad_normed = dot(grad_parts, w_project, (1, 1))
    grad_rows = grad_middle + backward_norm(grad_normed, unit_one, inverse_one, vectors[0])
    input_grad = give_back(grad_rows.astype(bf16))

    vector_grads = jnp.stack(
        [
            jnp.sum(grad_normed * unit_one, axis=0),
            jnp.sum(grad_normed, axis=0),
            jnp.sum(grad_attend.astype(f32), axis=0),
            jnp.sum(grad_normed_two * unit_two, axis=0),
            jnp.sum(grad_normed_two, axis=0),
            jnp.sum(seed_float, axis=0),
        ]
    )
    vector_grads = lax.dot_general(
        vector_grads,
        placed.astype(f32),
        (((1,), (1,)), ((), ())),
        precision=lax.Precision.HIGHEST,
        preferred_element_type=f32,
    )
    parts_sum = jnp.sum(grad_parts.astype(f32), axis=0).reshape(n_tp, 3, local_width)
    hidden_sum = jnp.sum(grad_hidden.astype(f32), axis=0).reshape(n_tp, ff_local)
    group_grads = jnp.concatenate([parts_sum[:, 0], parts_sum[:, 2], hidden_sum], axis=1)
    wanted = jnp.bitwise_xor(jnp.arange(n_tp, dtype=jnp.int32), z)
    wanted = (wanted % 2) * 2 + wanted // 2
    group_grads = jnp.take(group_grads, wanted, axis=0)
    total = jnp.concatenate([vector_grads.reshape(-1, depth), group_grads.reshape(-1, depth)])
    for step in (CORE, X, Y, Z_NEAR, Z_FAR):
        total = total + swapped(total, *step)
    split = 6 * width // depth
    own_vectors = lax.dynamic_index_in_dim(total[:split].reshape(6, -1, depth), place, 1, False)
    own_groups = lax.dynamic_index_in_dim(total[split:].reshape(n_tp, -1), z, 0, False)
    return (
        outputs,
        input_grad,
        own_vectors[0],
        own_vectors[1],
        grad_project.reshape(depth, 3, local_width),
        own_groups[: 2 * local_width].reshape(2, local_width),
        grad_output,
        own_vectors[2],
        own_vectors[3],
        own_vectors[4],
        grad_expand,
        own_groups[2 * local_width :],
        grad_shrink,
        own_vectors[5],
    )


def solution(mesh):
    one_image_each = mesh.shape["fsdp"] == 8 and mesh.shape["tp"] == 2 * CAP
    return jax.shard_map(
        per_device_whole_image if one_image_each else per_device,
        mesh=mesh,
        in_specs=(
            P("fsdp", "tp", None),
            P("fsdp", "tp", None),
            P("fsdp"),
            P("fsdp"),
            P("fsdp"),
            P("fsdp", None, "tp"),
            P(None, "tp"),
            P("tp", "fsdp"),
            P("fsdp"),
            P("fsdp"),
            P("fsdp"),
            P("fsdp", "tp"),
            P("tp"),
            P("tp", "fsdp"),
            P("fsdp"),
        ),
        out_specs=(
            P("fsdp", "tp", None),
            P("fsdp", "tp", None),
            P("fsdp"),
            P("fsdp"),
            P("fsdp", None, "tp"),
            P(None, "tp"),
            P("tp", "fsdp"),
            P("fsdp"),
            P("fsdp"),
            P("fsdp"),
            P("fsdp", "tp"),
            P("tp"),
            P("tp", "fsdp"),
            P("fsdp"),
        ),
        check_vma=False,
    )
```

```python
import jax
import jax.numpy as jnp
import numpy as np
from jax import lax
from jax.experimental import pallas as pl
from jax.experimental.pallas import tpu as pltpu
from jax.sharding import PartitionSpec as P

HEAD_DIM = 64
SEQ = 577
SEQ_PAD = 592
CAP = 2


epsilon = 1e-06


def forward_norm(values, norm_gain, norm_bias):
    average = jnp.mean(values, axis=-1, keepdims=True)
    centered = values - average
    variance = jnp.mean(centered * centered, axis=-1, keepdims=True)
    inverse = lax.rsqrt(variance + epsilon)
    unit = centered * inverse
    return (unit * norm_gain + norm_bias, unit, inverse)


def backward_norm(upstream, unit, inverse, norm_gain):
    scaled = upstream * norm_gain
    first = jnp.mean(scaled, axis=-1, keepdims=True)
    second = jnp.mean(scaled * unit, axis=-1, keepdims=True)
    return inverse * (scaled - first - unit * second)


def gelu_slope(hidden):
    return (
        0.5 * (1.0 + lax.erf(hidden * 0.7071067811865476))
        + hidden * jnp.exp(-0.5 * hidden * hidden) * 0.3989422804014327
    )


def attention_scores(queries, keys, factor, keylive):
    scores = (
        jnp.einsum("iqhd,ikhd->ihqk", queries, keys, preferred_element_type=jnp.float32) * factor
    )
    return jnp.where(keylive, scores, -1e30)


def per_device(
    inputs,
    cotangent,
    counts,
    first_gain,
    first_bias,
    query_key_value_weight,
    project_bias,
    output_weight,
    output_bias,
    second_gain,
    second_bias,
    expand_weight,
    expand_bias,
    shrink_weight,
    shrink_bias,
):
    local_rows = inputs.shape[1]
    local_width = query_key_value_weight.shape[2]
    local_heads = local_width // HEAD_DIM
    padded = SEQ_PAD
    all_rows = CAP * padded
    factor = HEAD_DIM ** (-0.5)
    vectors = jnp.stack(
        [first_gain, first_bias, output_bias, second_gain, second_bias, shrink_bias]
    )
    row_index = lax.axis_index("tp") * local_rows + jnp.arange(local_rows, dtype=jnp.int32)
    row_image = row_index // padded
    row_valid = row_index % padded < SEQ
    keylive = (jnp.arange(padded) < SEQ)[None, None, None, :]
    split_shape = (CAP, padded, local_heads, HEAD_DIM)
    qv_bias = project_bias.astype(jnp.float32)
    up_bias = expand_bias.astype(jnp.float32)

    def visit(totals, pieces):
        block_in, block_cot, count = pieces
        fetched = (
            lax.all_gather(query_key_value_weight, "fsdp", axis=0, tiled=True),
            lax.all_gather(output_weight, "fsdp", axis=1, tiled=True),
            lax.all_gather(expand_weight, "fsdp", axis=0, tiled=True),
            lax.all_gather(shrink_weight, "fsdp", axis=1, tiled=True),
            lax.all_gather(vectors, "fsdp", axis=1, tiled=True),
        )
        projection_weight_local, w_output, w_expand, w_shrink, vector_rows = fetched
        vector_rows = vector_rows.astype(jnp.float32)
        live = ((row_image < count) & row_valid).astype(jnp.float32)[:, None]
        block = block_in.astype(jnp.float32)
        normalized_rows, unit_one, inverse_one = forward_norm(block, vector_rows[0], vector_rows[1])
        first_token_rows = lax.all_gather(
            normalized_rows.astype(jnp.bfloat16), "tp", axis=0, tiled=True
        )
        projected_rows = jnp.einsum(
            "fk,kal->fal",
            first_token_rows,
            projection_weight_local,
            preferred_element_type=jnp.float32,
        )
        queries = (projected_rows[:, 0] + qv_bias[0]).astype(jnp.bfloat16).reshape(split_shape)
        keys = projected_rows[:, 1].astype(jnp.bfloat16).reshape(split_shape)
        values = (projected_rows[:, 2] + qv_bias[1]).astype(jnp.bfloat16).reshape(split_shape)
        scores = attention_scores(queries, keys, factor, keylive)
        row_peak = jnp.max(scores, axis=-1, keepdims=True)
        expon = jnp.exp(scores - row_peak)
        row_totals = jnp.sum(expon, axis=-1, keepdims=True)
        logsum = row_peak + jnp.log(row_totals)
        probs = (expon / row_totals).astype(jnp.bfloat16)
        mixed = (
            jnp.einsum("ihqk,ikhd->iqhd", probs, values, preferred_element_type=jnp.float32)
            .astype(jnp.bfloat16)
            .reshape(all_rows, local_width)
        )
        whole_output = lax.all_gather(w_output, "tp", axis=0, tiled=True)
        own_mixed = lax.all_to_all(mixed, "tp", split_axis=0, concat_axis=1, tiled=True)
        attend = jnp.dot(own_mixed, whole_output, preferred_element_type=jnp.float32)
        middle = block + attend + vector_rows[2]
        normed_two, unit_two, inverse_two = forward_norm(middle, vector_rows[3], vector_rows[4])
        tokens_two = lax.all_gather(normed_two.astype(jnp.bfloat16), "tp", axis=0, tiled=True)
        hidden = jnp.dot(tokens_two, w_expand, preferred_element_type=jnp.float32) + up_bias
        activated = jax.nn.gelu(hidden, approximate=False).astype(jnp.bfloat16)
        partial_two = jnp.dot(activated, w_shrink, preferred_element_type=jnp.float32)
        branch = lax.psum_scatter(
            partial_two.astype(jnp.bfloat16), "tp", scatter_dimension=0, tiled=True
        ).astype(jnp.float32)
        out_rows = ((middle + branch + vector_rows[5]) * live).astype(jnp.bfloat16)
        fetched_back = (
            lax.all_gather(query_key_value_weight, "fsdp", axis=0, tiled=True),
            lax.all_gather(output_weight, "fsdp", axis=1, tiled=True),
            lax.all_gather(expand_weight, "fsdp", axis=0, tiled=True),
            lax.all_gather(shrink_weight, "fsdp", axis=1, tiled=True),
            lax.all_gather(vectors, "fsdp", axis=1, tiled=True),
        )
        projection_back_local, b_output, b_expand, b_shrink, back_rows = fetched_back
        back_rows = back_rows.astype(jnp.float32)
        seed = (block_cot.astype(jnp.float32) * live).astype(jnp.bfloat16)
        seed_float = seed.astype(jnp.float32)
        seed_all = lax.all_gather(seed, "tp", axis=0, tiled=True)
        grad_shrink = jnp.einsum(
            "rf,rd->fd", activated, seed_all, preferred_element_type=jnp.float32
        )
        grad_hidden = (
            jnp.einsum("rd,fd->rf", seed_all, b_shrink, preferred_element_type=jnp.float32)
            * gelu_slope(hidden)
        ).astype(jnp.bfloat16)
        grad_expand = jnp.einsum(
            "rd,rf->df", tokens_two, grad_hidden, preferred_element_type=jnp.float32
        )
        grad_normed_two = lax.psum_scatter(
            jnp.einsum(
                "rf,df->rd", grad_hidden, b_expand, preferred_element_type=jnp.float32
            ).astype(jnp.bfloat16),
            "tp",
            scatter_dimension=0,
            tiled=True,
        ).astype(jnp.float32)
        grad_middle = seed_float + backward_norm(
            grad_normed_two, unit_two, inverse_two, back_rows[3]
        )
        grad_attend = grad_middle.astype(jnp.bfloat16)
        attend_all = lax.all_gather(grad_attend, "tp", axis=0, tiled=True)
        grad_output = jnp.einsum("re,rd->ed", mixed, attend_all, preferred_element_type=jnp.float32)
        grad_mixed = (
            jnp.einsum("rd,ed->re", attend_all, b_output, preferred_element_type=jnp.float32)
            .astype(jnp.bfloat16)
            .reshape(split_shape)
        )
        again = attention_scores(queries, keys, factor, keylive)
        probs_back = jnp.exp(again - logsum)
        grad_probs = jnp.einsum(
            "iqhd,ikhd->ihqk", grad_mixed, values, preferred_element_type=jnp.float32
        )
        inner = jnp.sum(grad_probs * probs_back, axis=-1, keepdims=True)
        grad_scores = (probs_back * (grad_probs - inner)).astype(jnp.bfloat16)
        grad_queries = (
            jnp.einsum("ihqk,ikhd->iqhd", grad_scores, keys, preferred_element_type=jnp.float32)
            * factor
        ).astype(jnp.bfloat16)
        grad_keys = (
            jnp.einsum("ihqk,iqhd->ikhd", grad_scores, queries, preferred_element_type=jnp.float32)
            * factor
        ).astype(jnp.bfloat16)
        grad_values = jnp.einsum(
            "ihqk,iqhd->ikhd",
            probs_back.astype(jnp.bfloat16),
            grad_mixed,
            preferred_element_type=jnp.float32,
        ).astype(jnp.bfloat16)
        stacked_rows = jnp.stack(
            [
                grad_queries.reshape(all_rows, local_width),
                grad_keys.reshape(all_rows, local_width),
                grad_values.reshape(all_rows, local_width),
            ],
            axis=1,
        )
        grad_project = jnp.einsum(
            "gz,gfo->zfo", first_token_rows, stacked_rows, preferred_element_type=jnp.float32
        )
        grad_normed = lax.psum_scatter(
            jnp.einsum(
                "inj,onj->io",
                stacked_rows,
                projection_back_local,
                preferred_element_type=jnp.float32,
            ).astype(jnp.bfloat16),
            "tp",
            scatter_dimension=0,
            tiled=True,
        ).astype(jnp.float32)
        grad_rows = (
            grad_middle + backward_norm(grad_normed, unit_one, inverse_one, back_rows[0])
        ).astype(jnp.bfloat16)
        vector_grads = jnp.stack(
            [
                jnp.sum(grad_normed * unit_one, axis=0),
                jnp.sum(grad_normed, axis=0),
                jnp.sum(grad_attend.astype(jnp.float32), axis=0),
                jnp.sum(grad_normed_two * unit_two, axis=0),
                jnp.sum(grad_normed_two, axis=0),
                jnp.sum(seed_float, axis=0),
            ]
        )
        qv_grads = jnp.sum(stacked_rows[:, 0::2].astype(jnp.float32), axis=0)
        up_grads = jnp.sum(grad_hidden.astype(jnp.float32), axis=0)
        updated = (
            totals[0] + grad_project,
            totals[1] + grad_output,
            totals[2] + grad_expand,
            totals[3] + grad_shrink,
            totals[4] + vector_grads,
            totals[5] + qv_grads,
            totals[6] + up_grads,
        )
        return (updated, (out_rows, grad_rows))

    width = inputs.shape[2]
    ff_local = expand_weight.shape[1]
    zeros = (
        jnp.zeros((width, 3, local_width), jnp.float32),
        jnp.zeros((local_width, width), jnp.float32),
        jnp.zeros((width, ff_local), jnp.float32),
        jnp.zeros((ff_local, width), jnp.float32),
        jnp.zeros((6, width), jnp.float32),
        jnp.zeros((2, local_width), jnp.float32),
        jnp.zeros((ff_local,), jnp.float32),
    )
    totals, (outputs, input_grad) = lax.scan(visit, zeros, (inputs, cotangent, counts))
    summed_vectors = lax.psum(totals[4], "tp")
    shards = (
        lax.psum_scatter(
            totals[0].astype(jnp.bfloat16), "fsdp", scatter_dimension=0, tiled=True
        ).astype(jnp.float32),
        lax.psum_scatter(
            totals[1].astype(jnp.bfloat16), "fsdp", scatter_dimension=1, tiled=True
        ).astype(jnp.float32),
        lax.psum_scatter(
            totals[2].astype(jnp.bfloat16), "fsdp", scatter_dimension=0, tiled=True
        ).astype(jnp.float32),
        lax.psum_scatter(
            totals[3].astype(jnp.bfloat16), "fsdp", scatter_dimension=1, tiled=True
        ).astype(jnp.float32),
        lax.psum_scatter(
            summed_vectors.astype(jnp.bfloat16), "fsdp", scatter_dimension=1, tiled=True
        ).astype(jnp.float32),
    )
    bias_totals = lax.psum((totals[5], totals[6]), "fsdp")
    vector_shards = shards[4]
    return (
        outputs,
        input_grad,
        vector_shards[0],
        vector_shards[1],
        shards[0],
        bias_totals[0],
        shards[1],
        vector_shards[2],
        vector_shards[3],
        vector_shards[4],
        shards[2],
        bias_totals[1],
        shards[3],
        vector_shards[5],
    )


def swapped(rows, axis, bit):
    size = lax.axis_size(axis)
    return lax.ppermute(rows, axis, [(i, i ^ bit) for i in range(size)])


CORE, X, Y = ("fsdp", 1), ("fsdp", 2), ("fsdp", 4)
Z_NEAR, Z_FAR = ("tp", 1), ("tp", 2)
WAYS = ((X, Y), (Y, X))


tie = lax.optimization_barrier


def gather_columns(part, step):
    return jnp.concatenate([part, swapped(part, *step)], axis=1)


def split_ways(part):
    half = part.shape[0] // 2
    return part[:half], part[half:]


def gather_ways(parts, leg):
    return tuple(
        jnp.concatenate([part, swapped(part, *way[leg])], axis=0) for part, way in zip(parts, WAYS)
    )


def gather_core(parts):
    own = jnp.concatenate(parts, axis=0)
    other = split_ways(swapped(own, *CORE))
    return jnp.concatenate([parts[0], other[0], parts[1], other[1]], axis=0)


def exchange_sum(kept, sent, step, kind=jnp.bfloat16):
    received = swapped(sent, *step)
    return (kept.astype(jnp.float32) + received.astype(jnp.float32)).astype(kind)


def scatter_core(grad):
    quarter = grad.shape[0] // 4
    piece = [grad[i * quarter : (i + 1) * quarter] for i in range(4)]
    received = split_ways(swapped(jnp.concatenate([piece[1], piece[3]], axis=0), *CORE))
    return tuple(
        (kept.astype(jnp.float32) + other.astype(jnp.float32)).astype(jnp.bfloat16)
        for kept, other in zip((piece[0], piece[2]), received)
    )


def scatter_ways(parts, leg):
    return tuple(exchange_sum(*split_ways(part), way[leg]) for part, way in zip(parts, WAYS))


def scatter_columns(part, step, kind=jnp.bfloat16):
    middle = part.shape[1] // 2
    return exchange_sum(part[:, :middle], part[:, middle:], step, kind)


def dot(left, right, contract):
    return lax.dot_general(
        left, right, ((contract[:1], contract[1:]), ((), ())), preferred_element_type=jnp.float32
    )


def head_probs(queries, keys, mask):
    scores = dot(queries, keys, (1, 1)) * HEAD_DIM ** (-0.5) + mask
    expon = jnp.exp(scores - jnp.max(scores, axis=-1, keepdims=True))
    return expon * (1.0 / jnp.sum(expon, axis=-1, keepdims=True))


def attend_kernel(mask_ref, project_ref, mixed_ref):
    width = mixed_ref.shape[1]
    mask = mask_ref[...]
    for head in range(width // HEAD_DIM):
        span = [slice(j * width + head * HEAD_DIM, j * width + (head + 1) * HEAD_DIM) for j in range(3)]
        queries, keys, values = (project_ref[:, s] for s in span)
        probs = head_probs(queries, keys, mask).astype(jnp.bfloat16)
        mixed_ref[:, span[0]] = dot(probs, values, (1, 0)).astype(jnp.bfloat16)


def attend_back_kernel(mask_ref, project_ref, grad_ref, out_ref):
    width = grad_ref.shape[1]
    mask = mask_ref[...]
    factor = HEAD_DIM ** (-0.5)
    for head in range(width // HEAD_DIM):
        span = [slice(j * width + head * HEAD_DIM, j * width + (head + 1) * HEAD_DIM) for j in range(3)]
        queries, keys, values = (project_ref[:, s] for s in span)
        grad_mixed = grad_ref[:, span[0]]
        probs = head_probs(queries, keys, mask)
        grad_probs = dot(grad_mixed, values, (1, 1))
        inner = jnp.sum(grad_probs * probs, axis=-1, keepdims=True)
        grad_scores = (probs * (grad_probs - inner)).astype(jnp.bfloat16)
        out_ref[:, span[0]] = (dot(grad_scores, keys, (1, 0)) * factor).astype(jnp.bfloat16)
        out_ref[:, span[1]] = (dot(grad_scores, queries, (0, 0)) * factor).astype(jnp.bfloat16)
        out_ref[:, span[2]] = dot(probs.astype(jnp.bfloat16), grad_mixed, (0, 0)).astype(jnp.bfloat16)


def attention_call(kernel, mask, operands, all_groups, base, groups, out_width, flops):
    rows = operands[0].shape[0]

    def block(width, base):
        return pl.BlockSpec((rows, width), lambda g: (0, g + base))

    return pl.pallas_call(
        kernel,
        grid=(groups,),
        in_specs=[pl.BlockSpec((1, rows), lambda g: (0, 0))]
        + [block(item.shape[1] // all_groups, base) for item in operands],
        out_specs=block(out_width // groups, 0),
        out_shape=jax.ShapeDtypeStruct((rows, out_width), jnp.bfloat16),
        compiler_params=pltpu.CompilerParams(vmem_limit_bytes=48 * 2**20),
        cost_estimate=pl.CostEstimate(
            flops=flops, bytes_accessed=8 * rows * out_width, transcendentals=0
        ),
    )(mask, *operands)


def per_device_whole_image(
    inputs,
    cotangent,
    counts,
    first_gain,
    first_bias,
    query_key_value_weight,
    project_bias,
    output_weight,
    output_bias,
    second_gain,
    second_bias,
    expand_weight,
    expand_bias,
    shrink_weight,
    shrink_bias,
):
    bf16, f32 = jnp.bfloat16, jnp.float32
    n_tp = lax.axis_size("tp")
    place, z = lax.axis_index("fsdp"), lax.axis_index("tp")
    odd = z % 2
    local_rows, width = inputs.shape[1:]
    depth, _, local_width = query_key_value_weight.shape
    ff_local = expand_weight.shape[1]
    rows = 2 * local_rows
    half = depth // 2

    core, first, second = (np.arange(8) >> 2) & 1, (np.arange(8) >> 1) & 1, np.arange(8) & 1
    relative = np.stack([second * 2 + first * 4 + core, first * 2 + second * 4 + core])
    offset = half * np.arange(2)[:, None, None] + np.arange(half)[None, None, :]
    absolute = (
        jnp.bitwise_xor(jnp.asarray(relative, jnp.int32), place)[:, :, None] * depth + offset
    ).reshape(width)
    placed = jnp.arange(width, dtype=jnp.int32)[:, None] == absolute[None, :]
    order = placed.astype(bf16)

    chain_one = query_key_value_weight.reshape(depth, 3 * local_width)
    chain_two = jnp.concatenate([output_weight.T, expand_weight], axis=1)
    chain_three = shrink_weight.T
    chain_one = gather_columns(chain_one, Z_FAR)
    chain_one, chain_two = tie((chain_one, chain_two))
    chain_one, chain_two = gather_columns(chain_one, Z_NEAR), gather_columns(chain_two, Z_FAR)
    chain_one, chain_two, chain_three = tie((chain_one, chain_two, chain_three))
    chain_one = gather_ways(split_ways(chain_one), 0)
    chain_two = gather_columns(chain_two, Z_NEAR)
    chain_three = gather_columns(chain_three, Z_FAR)
    chain_one, chain_two, chain_three = tie((chain_one, chain_two, chain_three))
    chain_one = gather_ways(chain_one, 1)
    chain_three = gather_columns(chain_three, Z_NEAR)
    chain_one, chain_two = tie((chain_one, chain_two))
    w_project = gather_core(chain_one)
    chain_two = gather_ways(split_ways(chain_two), 0)
    vectors = jnp.stack(
        [first_gain, first_bias, output_bias, second_gain, second_bias, shrink_bias]
    ).reshape(6, 1, depth)
    for step in (X, Y, CORE):
        vectors = jnp.concatenate([vectors, swapped(vectors, *step)], axis=1)
    vectors = vectors.reshape(6, 2, 2, 2, 2, half)
    vectors = jnp.stack(
        [vectors[:, :, :, :, 0], jnp.swapaxes(vectors[:, :, :, :, 1], 2, 3)], axis=1
    ).reshape(6, 1, width).astype(f32)
    biases = jnp.concatenate([project_bias.reshape(1, -1), expand_bias[None]], axis=1)
    for step in (Z_FAR, Z_NEAR):
        biases = jnp.concatenate([biases, swapped(biases, *step)], axis=0)
    biases = biases.astype(f32)
    zero = jnp.zeros((n_tp, local_width), f32)
    qkv_bias = jnp.stack(
        [biases[:, :local_width], zero, biases[:, local_width : 2 * local_width]], axis=1
    ).reshape(1, -1)
    up_bias = biases[:, 2 * local_width :].reshape(1, -1)

    def fetch(whole):
        own = jnp.where(odd == 0, whole[0], whole[1])
        other = jnp.where(odd == 0, whole[1], whole[0])
        taken = jnp.concatenate([own, swapped(other, *Z_NEAR)], axis=0)
        return dot(taken, order, (1, 0))

    def give_back(taken):
        taken = dot(taken, order, (1, 1)).astype(bf16)
        own, other = taken[:local_rows], swapped(taken[local_rows:], *Z_NEAR)
        return jnp.where(odd == 0, jnp.stack([own, other]), jnp.stack([other, own]))

    index = jnp.arange(rows, dtype=jnp.int32)
    position = jnp.where(odd == 1, (index + local_rows) % rows, index)
    count = jnp.where(odd == 0, counts[0], counts[1])
    live = ((position < SEQ) & (z // 2 < count)).astype(f32)[:, None]
    mask = jnp.where(position < SEQ, 0.0, -1e30).astype(f32)[None]

    block = fetch(inputs)
    seed_float = fetch(cotangent) * live
    seed = seed_float.astype(bf16)

    normed_one, unit_one, inverse_one = forward_norm(block, vectors[0], vectors[1])
    normed_one = normed_one.astype(bf16)
    project = (dot(normed_one, w_project, (1, 0)) + qkv_bias).astype(bf16)
    pair_flops = 2 * rows * rows * width
    project, chain_two, chain_three = tie((project, chain_two, chain_three))
    mixed = attention_call(attend_kernel, mask, [project], n_tp, 0, n_tp, width, 2 * pair_flops)
    chain_two = gather_ways(chain_two, 1)
    chain_three = gather_ways(split_ways(chain_three), 0)
    mixed, chain_two, chain_three = tie((mixed, chain_two, chain_three))
    chain_two = gather_core(chain_two)
    chain_three = gather_ways(chain_three, 1)
    group = local_width + ff_local
    starts = range(0, n_tp * group, group)
    w_output = jnp.concatenate([chain_two[:, i : i + local_width] for i in starts], axis=1)
    w_expand = jnp.concatenate([chain_two[:, i + local_width : i + group] for i in starts], axis=1)
    middle = block + dot(mixed, w_output, (1, 1)) + vectors[2]
    normed_two, unit_two, inverse_two = forward_norm(middle, vectors[3], vectors[4])
    normed_two, chain_three = tie((normed_two.astype(bf16), chain_three))
    w_shrink = gather_core(chain_three)
    hidden = dot(normed_two, w_expand, (1, 0)) + up_bias
    activated = jax.nn.gelu(hidden, approximate=False).astype(bf16)

    scatter_one = dot(seed, activated, (0, 0)).astype(bf16)
    scatter_one, activated, w_shrink = tie((scatter_one, activated, w_shrink))
    scatter_one = scatter_core(scatter_one)
    branch = dot(activated, w_shrink, (1, 1))
    outputs = give_back(((middle + branch + vectors[5]) * live).astype(bf16))
    grad_hidden = (dot(seed, w_shrink, (1, 0)) * gelu_slope(hidden)).astype(bf16)
    scatter_one, grad_hidden = tie((scatter_one, grad_hidden))
    scatter_one = scatter_ways(scatter_one, 1)
    grad_expand = dot(normed_two, grad_hidden, (0, 0)).astype(bf16)
    grad_normed_two = dot(grad_hidden, w_expand, (1, 1))
    grad_middle = seed_float + backward_norm(grad_normed_two, unit_two, inverse_two, vectors[3])
    grad_attend = grad_middle.astype(bf16)
    scatter_one, grad_attend, grad_expand = tie((scatter_one, grad_attend, grad_expand))
    scatter_one = scatter_ways(scatter_one, 0)
    grad_output = dot(grad_attend, mixed, (0, 0)).astype(bf16)
    grad_mixed = dot(grad_attend, w_output, (1, 0)).astype(bf16)
    scatter_two = jnp.concatenate(
        [
            item[:, g * size : (g + 1) * size]
            for g in range(n_tp)
            for item, size in ((grad_output, local_width), (grad_expand, ff_local))
        ],
        axis=1,
    )
    scatter_one, scatter_two, grad_mixed = tie((scatter_one, scatter_two, grad_mixed))
    scatter_one = scatter_columns(jnp.concatenate(scatter_one, axis=0), Z_NEAR)
    scatter_two = scatter_core(scatter_two)

    def attend_back(base, grad_mixed):
        return attention_call(
            attend_back_kernel,
            mask,
            [project, grad_mixed],
            n_tp,
            base,
            n_tp // 2,
            3 * width // 2,
            5 * pair_flops // 2,
        )

    early_parts = attend_back(0, grad_mixed)
    early_parts, grad_mixed, scatter_one, scatter_two = tie(
        (early_parts, grad_mixed, scatter_one, scatter_two)
    )
    scatter_one = scatter_columns(scatter_one, Z_FAR, f32)
    scatter_two = scatter_ways(scatter_two, 1)
    grad_parts = jnp.concatenate([early_parts, attend_back(n_tp // 2, grad_mixed)], axis=1)
    scatter_three = dot(normed_one, grad_parts, (0, 0)).astype(bf16)
    scatter_three, grad_parts, scatter_two, scatter_one = tie(
        (scatter_three, grad_parts, scatter_two, scatter_one)
    )
    grad_shrink = scatter_one.T
    scatter_three = scatter_core(scatter_three)
    scatter_two = scatter_ways(scatter_two, 0)
    grad_normed = dot(grad_parts, w_project, (1, 1))
    scatter_three, grad_normed, scatter_two = tie((scatter_three, grad_normed, scatter_two))
    scatter_three = scatter_ways(scatter_three, 1)
    scatter_two = scatter_columns(jnp.concatenate(scatter_two, axis=0), Z_NEAR)
    grad_rows = grad_middle + backward_norm(grad_normed, unit_one, inverse_one, vectors[0])
    input_grad = give_back(grad_rows.astype(bf16))
    scatter_three, scatter_two = tie((scatter_three, scatter_two))
    scatter_three = scatter_ways(scatter_three, 0)
    scatter_two = scatter_columns(scatter_two, Z_FAR, f32)
    scatter_three = scatter_columns(jnp.concatenate(scatter_three, axis=0), Z_NEAR)
    grad_project = scatter_columns(scatter_three, Z_FAR, f32)
    grad_output, grad_expand = scatter_two[:, :local_width].T, scatter_two[:, local_width:]

    vector_grads = jnp.stack(
        [
            jnp.sum(grad_normed * unit_one, axis=0),
            jnp.sum(grad_normed, axis=0),
            jnp.sum(grad_attend.astype(f32), axis=0),
            jnp.sum(grad_normed_two * unit_two, axis=0),
            jnp.sum(grad_normed_two, axis=0),
            jnp.sum(seed_float, axis=0),
        ]
    )
    vector_grads = lax.dot_general(
        vector_grads,
        placed.astype(f32),
        (((1,), (1,)), ((), ())),
        precision=lax.Precision.HIGHEST,
        preferred_element_type=f32,
    )
    parts_sum = jnp.sum(grad_parts.astype(f32), axis=0).reshape(n_tp, 3, local_width)
    hidden_sum = jnp.sum(grad_hidden.astype(f32), axis=0).reshape(n_tp, ff_local)
    group_grads = jnp.concatenate([parts_sum[:, 0], parts_sum[:, 2], hidden_sum], axis=1)
    wanted = jnp.bitwise_xor(jnp.arange(n_tp, dtype=jnp.int32), z)
    wanted = (wanted % 2) * 2 + wanted // 2
    group_grads = jnp.take(group_grads, wanted, axis=0)
    total = jnp.concatenate([vector_grads.reshape(-1, depth), group_grads.reshape(-1, depth)])
    for step in (CORE, X, Y, Z_NEAR, Z_FAR):
        total = total + swapped(total, *step)
    split = 6 * width // depth
    own_vectors = lax.dynamic_index_in_dim(total[:split].reshape(6, -1, depth), place, 1, False)
    own_groups = lax.dynamic_index_in_dim(total[split:].reshape(n_tp, -1), z, 0, False)
    return (
        outputs,
        input_grad,
        own_vectors[0],
        own_vectors[1],
        grad_project.reshape(depth, 3, local_width),
        own_groups[: 2 * local_width].reshape(2, local_width),
        grad_output,
        own_vectors[2],
        own_vectors[3],
        own_vectors[4],
        grad_expand,
        own_groups[2 * local_width :],
        grad_shrink,
        own_vectors[5],
    )


def solution(mesh):
    one_image_each = mesh.shape["fsdp"] == 8 and mesh.shape["tp"] == 2 * CAP
    return jax.shard_map(
        per_device_whole_image if one_image_each else per_device,
        mesh=mesh,
        in_specs=(
            P("fsdp", "tp", None),
            P("fsdp", "tp", None),
            P("fsdp"),
            P("fsdp"),
            P("fsdp"),
            P("fsdp", None, "tp"),
            P(None, "tp"),
            P("tp", "fsdp"),
            P("fsdp"),
            P("fsdp"),
            P("fsdp"),
            P("fsdp", "tp"),
            P("tp"),
            P("tp", "fsdp"),
            P("fsdp"),
        ),
        out_specs=(
            P("fsdp", "tp", None),
            P("fsdp", "tp", None),
            P("fsdp"),
            P("fsdp"),
            P("fsdp", None, "tp"),
            P(None, "tp"),
            P("tp", "fsdp"),
            P("fsdp"),
            P("fsdp"),
            P("fsdp"),
            P("fsdp", "tp"),
            P("tp"),
            P("tp", "fsdp"),
            P("fsdp"),
        ),
        check_vma=False,
    )
```

```python
import jax
import jax.numpy as jnp
import numpy as np
from jax import lax
from jax.experimental import pallas as pl
from jax.experimental.pallas import tpu as pltpu
from jax.sharding import PartitionSpec as P

HEAD_DIM = 64
SEQ = 577
SEQ_PAD = 592
CAP = 2


epsilon = 1e-06


def forward_norm(values, norm_gain, norm_bias):
    average = jnp.mean(values, axis=-1, keepdims=True)
    centered = values - average
    variance = jnp.mean(centered * centered, axis=-1, keepdims=True)
    inverse = lax.rsqrt(variance + epsilon)
    unit = centered * inverse
    return (unit * norm_gain + norm_bias, unit, inverse)


def backward_norm(upstream, unit, inverse, norm_gain):
    scaled = upstream * norm_gain
    first = jnp.mean(scaled, axis=-1, keepdims=True)
    second = jnp.mean(scaled * unit, axis=-1, keepdims=True)
    return inverse * (scaled - first - unit * second)


def gelu_slope(hidden):
    return (
        0.5 * (1.0 + lax.erf(hidden * 0.7071067811865476))
        + hidden * jnp.exp(-0.5 * hidden * hidden) * 0.3989422804014327
    )


def attention_scores(queries, keys, factor, keylive):
    scores = (
        jnp.einsum("iqhd,ikhd->ihqk", queries, keys, preferred_element_type=jnp.float32) * factor
    )
    return jnp.where(keylive, scores, -1e30)


def per_device(
    inputs,
    cotangent,
    counts,
    first_gain,
    first_bias,
    query_key_value_weight,
    project_bias,
    output_weight,
    output_bias,
    second_gain,
    second_bias,
    expand_weight,
    expand_bias,
    shrink_weight,
    shrink_bias,
):
    local_rows = inputs.shape[1]
    local_width = query_key_value_weight.shape[2]
    local_heads = local_width // HEAD_DIM
    padded = SEQ_PAD
    all_rows = CAP * padded
    factor = HEAD_DIM ** (-0.5)
    vectors = jnp.stack(
        [first_gain, first_bias, output_bias, second_gain, second_bias, shrink_bias]
    )
    row_index = lax.axis_index("tp") * local_rows + jnp.arange(local_rows, dtype=jnp.int32)
    row_image = row_index // padded
    row_valid = row_index % padded < SEQ
    keylive = (jnp.arange(padded) < SEQ)[None, None, None, :]
    split_shape = (CAP, padded, local_heads, HEAD_DIM)
    qv_bias = project_bias.astype(jnp.float32)
    up_bias = expand_bias.astype(jnp.float32)

    def visit(totals, pieces):
        block_in, block_cot, count = pieces
        fetched = (
            lax.all_gather(query_key_value_weight, "fsdp", axis=0, tiled=True),
            lax.all_gather(output_weight, "fsdp", axis=1, tiled=True),
            lax.all_gather(expand_weight, "fsdp", axis=0, tiled=True),
            lax.all_gather(shrink_weight, "fsdp", axis=1, tiled=True),
            lax.all_gather(vectors, "fsdp", axis=1, tiled=True),
        )
        projection_weight_local, w_output, w_expand, w_shrink, vector_rows = fetched
        vector_rows = vector_rows.astype(jnp.float32)
        live = ((row_image < count) & row_valid).astype(jnp.float32)[:, None]
        block = block_in.astype(jnp.float32)
        normalized_rows, unit_one, inverse_one = forward_norm(block, vector_rows[0], vector_rows[1])
        first_token_rows = lax.all_gather(
            normalized_rows.astype(jnp.bfloat16), "tp", axis=0, tiled=True
        )
        projected_rows = jnp.einsum(
            "fk,kal->fal",
            first_token_rows,
            projection_weight_local,
            preferred_element_type=jnp.float32,
        )
        queries = (projected_rows[:, 0] + qv_bias[0]).astype(jnp.bfloat16).reshape(split_shape)
        keys = projected_rows[:, 1].astype(jnp.bfloat16).reshape(split_shape)
        values = (projected_rows[:, 2] + qv_bias[1]).astype(jnp.bfloat16).reshape(split_shape)
        scores = attention_scores(queries, keys, factor, keylive)
        row_peak = jnp.max(scores, axis=-1, keepdims=True)
        expon = jnp.exp(scores - row_peak)
        row_totals = jnp.sum(expon, axis=-1, keepdims=True)
        logsum = row_peak + jnp.log(row_totals)
        probs = (expon / row_totals).astype(jnp.bfloat16)
        mixed = (
            jnp.einsum("ihqk,ikhd->iqhd", probs, values, preferred_element_type=jnp.float32)
            .astype(jnp.bfloat16)
            .reshape(all_rows, local_width)
        )
        whole_output = lax.all_gather(w_output, "tp", axis=0, tiled=True)
        own_mixed = lax.all_to_all(mixed, "tp", split_axis=0, concat_axis=1, tiled=True)
        attend = jnp.dot(own_mixed, whole_output, preferred_element_type=jnp.float32)
        middle = block + attend + vector_rows[2]
        normed_two, unit_two, inverse_two = forward_norm(middle, vector_rows[3], vector_rows[4])
        tokens_two = lax.all_gather(normed_two.astype(jnp.bfloat16), "tp", axis=0, tiled=True)
        hidden = jnp.dot(tokens_two, w_expand, preferred_element_type=jnp.float32) + up_bias
        activated = jax.nn.gelu(hidden, approximate=False).astype(jnp.bfloat16)
        partial_two = jnp.dot(activated, w_shrink, preferred_element_type=jnp.float32)
        branch = lax.psum_scatter(
            partial_two.astype(jnp.bfloat16), "tp", scatter_dimension=0, tiled=True
        ).astype(jnp.float32)
        out_rows = ((middle + branch + vector_rows[5]) * live).astype(jnp.bfloat16)
        fetched_back = (
            lax.all_gather(query_key_value_weight, "fsdp", axis=0, tiled=True),
            lax.all_gather(output_weight, "fsdp", axis=1, tiled=True),
            lax.all_gather(expand_weight, "fsdp", axis=0, tiled=True),
            lax.all_gather(shrink_weight, "fsdp", axis=1, tiled=True),
            lax.all_gather(vectors, "fsdp", axis=1, tiled=True),
        )
        projection_back_local, b_output, b_expand, b_shrink, back_rows = fetched_back
        back_rows = back_rows.astype(jnp.float32)
        seed = (block_cot.astype(jnp.float32) * live).astype(jnp.bfloat16)
        seed_float = seed.astype(jnp.float32)
        seed_all = lax.all_gather(seed, "tp", axis=0, tiled=True)
        grad_shrink = jnp.einsum(
            "rf,rd->fd", activated, seed_all, preferred_element_type=jnp.float32
        )
        grad_hidden = (
            jnp.einsum("rd,fd->rf", seed_all, b_shrink, preferred_element_type=jnp.float32)
            * gelu_slope(hidden)
        ).astype(jnp.bfloat16)
        grad_expand = jnp.einsum(
            "rd,rf->df", tokens_two, grad_hidden, preferred_element_type=jnp.float32
        )
        grad_normed_two = lax.psum_scatter(
            jnp.einsum(
                "rf,df->rd", grad_hidden, b_expand, preferred_element_type=jnp.float32
            ).astype(jnp.bfloat16),
            "tp",
            scatter_dimension=0,
            tiled=True,
        ).astype(jnp.float32)
        grad_middle = seed_float + backward_norm(
            grad_normed_two, unit_two, inverse_two, back_rows[3]
        )
        grad_attend = grad_middle.astype(jnp.bfloat16)
        attend_all = lax.all_gather(grad_attend, "tp", axis=0, tiled=True)
        grad_output = jnp.einsum("re,rd->ed", mixed, attend_all, preferred_element_type=jnp.float32)
        grad_mixed = (
            jnp.einsum("rd,ed->re", attend_all, b_output, preferred_element_type=jnp.float32)
            .astype(jnp.bfloat16)
            .reshape(split_shape)
        )
        again = attention_scores(queries, keys, factor, keylive)
        probs_back = jnp.exp(again - logsum)
        grad_probs = jnp.einsum(
            "iqhd,ikhd->ihqk", grad_mixed, values, preferred_element_type=jnp.float32
        )
        inner = jnp.sum(grad_probs * probs_back, axis=-1, keepdims=True)
        grad_scores = (probs_back * (grad_probs - inner)).astype(jnp.bfloat16)
        grad_queries = (
            jnp.einsum("ihqk,ikhd->iqhd", grad_scores, keys, preferred_element_type=jnp.float32)
            * factor
        ).astype(jnp.bfloat16)
        grad_keys = (
            jnp.einsum("ihqk,iqhd->ikhd", grad_scores, queries, preferred_element_type=jnp.float32)
            * factor
        ).astype(jnp.bfloat16)
        grad_values = jnp.einsum(
            "ihqk,iqhd->ikhd",
            probs_back.astype(jnp.bfloat16),
            grad_mixed,
            preferred_element_type=jnp.float32,
        ).astype(jnp.bfloat16)
        stacked_rows = jnp.stack(
            [
                grad_queries.reshape(all_rows, local_width),
                grad_keys.reshape(all_rows, local_width),
                grad_values.reshape(all_rows, local_width),
            ],
            axis=1,
        )
        grad_project = jnp.einsum(
            "gz,gfo->zfo", first_token_rows, stacked_rows, preferred_element_type=jnp.float32
        )
        grad_normed = lax.psum_scatter(
            jnp.einsum(
                "inj,onj->io",
                stacked_rows,
                projection_back_local,
                preferred_element_type=jnp.float32,
            ).astype(jnp.bfloat16),
            "tp",
            scatter_dimension=0,
            tiled=True,
        ).astype(jnp.float32)
        grad_rows = (
            grad_middle + backward_norm(grad_normed, unit_one, inverse_one, back_rows[0])
        ).astype(jnp.bfloat16)
        vector_grads = jnp.stack(
            [
                jnp.sum(grad_normed * unit_one, axis=0),
                jnp.sum(grad_normed, axis=0),
                jnp.sum(grad_attend.astype(jnp.float32), axis=0),
                jnp.sum(grad_normed_two * unit_two, axis=0),
                jnp.sum(grad_normed_two, axis=0),
                jnp.sum(seed_float, axis=0),
            ]
        )
        qv_grads = jnp.sum(stacked_rows[:, 0::2].astype(jnp.float32), axis=0)
        up_grads = jnp.sum(grad_hidden.astype(jnp.float32), axis=0)
        updated = (
            totals[0] + grad_project,
            totals[1] + grad_output,
            totals[2] + grad_expand,
            totals[3] + grad_shrink,
            totals[4] + vector_grads,
            totals[5] + qv_grads,
            totals[6] + up_grads,
        )
        return (updated, (out_rows, grad_rows))

    width = inputs.shape[2]
    ff_local = expand_weight.shape[1]
    zeros = (
        jnp.zeros((width, 3, local_width), jnp.float32),
        jnp.zeros((local_width, width), jnp.float32),
        jnp.zeros((width, ff_local), jnp.float32),
        jnp.zeros((ff_local, width), jnp.float32),
        jnp.zeros((6, width), jnp.float32),
        jnp.zeros((2, local_width), jnp.float32),
        jnp.zeros((ff_local,), jnp.float32),
    )
    totals, (outputs, input_grad) = lax.scan(visit, zeros, (inputs, cotangent, counts))
    summed_vectors = lax.psum(totals[4], "tp")
    shards = (
        lax.psum_scatter(
            totals[0].astype(jnp.bfloat16), "fsdp", scatter_dimension=0, tiled=True
        ).astype(jnp.float32),
        lax.psum_scatter(
            totals[1].astype(jnp.bfloat16), "fsdp", scatter_dimension=1, tiled=True
        ).astype(jnp.float32),
        lax.psum_scatter(
            totals[2].astype(jnp.bfloat16), "fsdp", scatter_dimension=0, tiled=True
        ).astype(jnp.float32),
        lax.psum_scatter(
            totals[3].astype(jnp.bfloat16), "fsdp", scatter_dimension=1, tiled=True
        ).astype(jnp.float32),
        lax.psum_scatter(
            summed_vectors.astype(jnp.bfloat16), "fsdp", scatter_dimension=1, tiled=True
        ).astype(jnp.float32),
    )
    bias_totals = lax.psum((totals[5], totals[6]), "fsdp")
    vector_shards = shards[4]
    return (
        outputs,
        input_grad,
        vector_shards[0],
        vector_shards[1],
        shards[0],
        bias_totals[0],
        shards[1],
        vector_shards[2],
        vector_shards[3],
        vector_shards[4],
        shards[2],
        bias_totals[1],
        shards[3],
        vector_shards[5],
    )


def swapped(rows, axis, bit):
    size = lax.axis_size(axis)
    return lax.ppermute(rows, axis, [(i, i ^ bit) for i in range(size)])


CORE, X, Y = ("fsdp", 1), ("fsdp", 2), ("fsdp", 4)
Z_NEAR, Z_FAR = ("tp", 1), ("tp", 2)
WAYS = ((X, Y), (Y, X))


tie = lax.optimization_barrier


def gather_columns(part, step):
    return jnp.concatenate([part, swapped(part, *step)], axis=1)


def split_ways(part):
    half = part.shape[0] // 2
    return part[:half], part[half:]


def gather_ways(parts, leg):
    return tuple(
        jnp.concatenate([part, swapped(part, *way[leg])], axis=0) for part, way in zip(parts, WAYS)
    )


def gather_core(parts):
    own = jnp.concatenate(parts, axis=0)
    other = split_ways(swapped(own, *CORE))
    return jnp.concatenate([parts[0], other[0], parts[1], other[1]], axis=0)


def exchange_sum(kept, sent, step, kind=jnp.bfloat16):
    received = swapped(sent, *step)
    return (kept.astype(jnp.float32) + received.astype(jnp.float32)).astype(kind)


def scatter_core(grad):
    quarter = grad.shape[0] // 4
    piece = [grad[i * quarter : (i + 1) * quarter] for i in range(4)]
    received = split_ways(swapped(jnp.concatenate([piece[1], piece[3]], axis=0), *CORE))
    return tuple(
        (kept.astype(jnp.float32) + other.astype(jnp.float32)).astype(jnp.bfloat16)
        for kept, other in zip((piece[0], piece[2]), received)
    )


def scatter_ways(parts, leg):
    return tuple(exchange_sum(*split_ways(part), way[leg]) for part, way in zip(parts, WAYS))


def scatter_columns(part, step, kind=jnp.bfloat16):
    middle = part.shape[1] // 2
    return exchange_sum(part[:, :middle], part[:, middle:], step, kind)


def dot(left, right, contract):
    return lax.dot_general(
        left, right, ((contract[:1], contract[1:]), ((), ())), preferred_element_type=jnp.float32
    )


def head_probs(queries, keys, mask):
    scores = dot(queries, keys, (1, 1)) * HEAD_DIM ** (-0.5) + mask
    expon = jnp.exp(scores - jnp.max(scores, axis=-1, keepdims=True))
    return expon * (1.0 / jnp.sum(expon, axis=-1, keepdims=True))


def attend_kernel(mask_ref, project_ref, mixed_ref):
    width = mixed_ref.shape[1]
    mask = mask_ref[...]
    for head in range(width // HEAD_DIM):
        span = [slice(j * width + head * HEAD_DIM, j * width + (head + 1) * HEAD_DIM) for j in range(3)]
        queries, keys, values = (project_ref[:, s] for s in span)
        probs = head_probs(queries, keys, mask).astype(jnp.bfloat16)
        mixed_ref[:, span[0]] = dot(probs, values, (1, 0)).astype(jnp.bfloat16)


def attend_back_kernel(mask_ref, project_ref, grad_ref, out_ref):
    width = grad_ref.shape[1]
    mask = mask_ref[...]
    factor = HEAD_DIM ** (-0.5)
    for head in range(width // HEAD_DIM):
        span = [slice(j * width + head * HEAD_DIM, j * width + (head + 1) * HEAD_DIM) for j in range(3)]
        queries, keys, values = (project_ref[:, s] for s in span)
        grad_mixed = grad_ref[:, span[0]]
        probs = head_probs(queries, keys, mask)
        grad_probs = dot(grad_mixed, values, (1, 1))
        inner = jnp.sum(grad_probs * probs, axis=-1, keepdims=True)
        grad_scores = (probs * (grad_probs - inner)).astype(jnp.bfloat16)
        out_ref[:, span[0]] = (dot(grad_scores, keys, (1, 0)) * factor).astype(jnp.bfloat16)
        out_ref[:, span[1]] = (dot(grad_scores, queries, (0, 0)) * factor).astype(jnp.bfloat16)
        out_ref[:, span[2]] = dot(probs.astype(jnp.bfloat16), grad_mixed, (0, 0)).astype(jnp.bfloat16)


def attention_call(kernel, mask, operands, all_groups, base, groups, out_width, flops):
    rows = operands[0].shape[0]

    def block(width, base):
        return pl.BlockSpec((rows, width), lambda g: (0, g + base))

    return pl.pallas_call(
        kernel,
        grid=(groups,),
        in_specs=[pl.BlockSpec((1, rows), lambda g: (0, 0))]
        + [block(item.shape[1] // all_groups, base) for item in operands],
        out_specs=block(out_width // groups, 0),
        out_shape=jax.ShapeDtypeStruct((rows, out_width), jnp.bfloat16),
        compiler_params=pltpu.CompilerParams(vmem_limit_bytes=48 * 2**20),
        cost_estimate=pl.CostEstimate(
            flops=flops, bytes_accessed=8 * rows * out_width, transcendentals=0
        ),
    )(mask, *operands)


def per_device_whole_image(
    inputs,
    cotangent,
    counts,
    first_gain,
    first_bias,
    query_key_value_weight,
    project_bias,
    output_weight,
    output_bias,
    second_gain,
    second_bias,
    expand_weight,
    expand_bias,
    shrink_weight,
    shrink_bias,
):
    bf16, f32 = jnp.bfloat16, jnp.float32
    n_tp = lax.axis_size("tp")
    place, z = lax.axis_index("fsdp"), lax.axis_index("tp")
    odd = z % 2
    local_rows, width = inputs.shape[1:]
    depth, _, local_width = query_key_value_weight.shape
    ff_local = expand_weight.shape[1]
    rows = 2 * local_rows
    half = depth // 2

    core, first, second = (np.arange(8) >> 2) & 1, (np.arange(8) >> 1) & 1, np.arange(8) & 1
    relative = np.stack([second * 2 + first * 4 + core, first * 2 + second * 4 + core])
    offset = half * np.arange(2)[:, None, None] + np.arange(half)[None, None, :]
    absolute = (
        jnp.bitwise_xor(jnp.asarray(relative, jnp.int32), place)[:, :, None] * depth + offset
    ).reshape(width)
    placed = jnp.arange(width, dtype=jnp.int32)[:, None] == absolute[None, :]
    order = placed.astype(bf16)

    chain_one = query_key_value_weight.reshape(depth, 3 * local_width)
    chain_two = (output_weight.T, expand_weight)
    chain_three = shrink_weight.T
    chain_one = gather_columns(chain_one, Z_FAR)
    chain_one, chain_two = tie((chain_one, chain_two))
    chain_one = gather_columns(chain_one, Z_NEAR)
    chain_two = tuple(gather_columns(part, Z_FAR) for part in chain_two)
    chain_one, chain_two, chain_three, inputs = tie((chain_one, chain_two, chain_three, inputs))
    chain_one = gather_ways(split_ways(chain_one), 0)
    chain_two = jnp.concatenate([gather_columns(part, Z_NEAR) for part in chain_two], axis=1)
    chain_three = gather_columns(chain_three, Z_FAR)
    vectors = jnp.stack(
        [first_gain, first_bias, output_bias, second_gain, second_bias, shrink_bias]
    ).reshape(6, 1, depth)
    biases = jnp.concatenate([project_bias.reshape(1, -1), expand_bias[None]], axis=1)
    chain_one, chain_two, chain_three, vectors, biases = tie(
        (chain_one, chain_two, chain_three, vectors, biases)
    )
    chain_one = gather_ways(chain_one, 1)
    chain_three = gather_columns(chain_three, Z_NEAR)
    chain_one, chain_two = tie((chain_one, chain_two))
    w_project = gather_core(chain_one)
    chain_two = gather_ways(split_ways(chain_two), 0)
    for step in (X, Y, CORE):
        vectors = jnp.concatenate([vectors, swapped(vectors, *step)], axis=1)
    vectors = vectors.reshape(6, 2, 2, 2, 2, half)
    vectors = jnp.stack(
        [vectors[:, :, :, :, 0], jnp.swapaxes(vectors[:, :, :, :, 1], 2, 3)], axis=1
    ).reshape(6, 1, width).astype(f32)
    for step in (Z_FAR, Z_NEAR):
        biases = jnp.concatenate([biases, swapped(biases, *step)], axis=0)
    biases = biases.astype(f32)
    zero = jnp.zeros((n_tp, local_width), f32)
    qkv_bias = jnp.stack(
        [biases[:, :local_width], zero, biases[:, local_width : 2 * local_width]], axis=1
    ).reshape(1, -1)
    up_bias = biases[:, 2 * local_width :].reshape(1, -1)

    def exchanged(whole):
        own = jnp.where(odd == 0, whole[0], whole[1])
        other = jnp.where(odd == 0, whole[1], whole[0])
        return own, swapped(other, *Z_NEAR)

    def fetch(halves):
        return dot(jnp.concatenate(halves, axis=0), order, (1, 0))

    def give_back(taken):
        taken = dot(taken, order, (1, 1)).astype(bf16)
        return taken[:local_rows], swapped(taken[local_rows:], *Z_NEAR)

    def restored(own, other):
        return jnp.where(odd == 0, jnp.stack([own, other]), jnp.stack([other, own]))

    index = jnp.arange(rows, dtype=jnp.int32)
    position = jnp.where(odd == 1, (index + local_rows) % rows, index)
    count = jnp.where(odd == 0, counts[0], counts[1])
    live = ((position < SEQ) & (z // 2 < count)).astype(f32)[:, None]
    mask = jnp.where(position < SEQ, 0.0, -1e30).astype(f32)[None]

    block = fetch(exchanged(inputs))

    normed_one, unit_one, inverse_one = forward_norm(block, vectors[0], vectors[1])
    normed_one = normed_one.astype(bf16)
    project = (dot(normed_one, w_project, (1, 0)) + qkv_bias).astype(bf16)
    pair_flops = 2 * rows * rows * width
    project, chain_two, chain_three, cotangent = tie(
        (project, chain_two, chain_three, cotangent)
    )
    cotangent = exchanged(cotangent)
    mixed = attention_call(attend_kernel, mask, [project], n_tp, 0, n_tp, width, 2 * pair_flops)
    chain_two = gather_ways(chain_two, 1)
    chain_three = gather_ways(split_ways(chain_three), 0)
    mixed, chain_two, chain_three, cotangent = tie((mixed, chain_two, chain_three, cotangent))
    seed_float = fetch(cotangent) * live
    seed = seed_float.astype(bf16)
    chain_two = gather_core(chain_two)
    chain_three = gather_ways(chain_three, 1)
    w_output, w_expand = chain_two[:, :width], chain_two[:, width:]
    middle = block + dot(mixed, w_output, (1, 1)) + vectors[2]
    normed_two, unit_two, inverse_two = forward_norm(middle, vectors[3], vectors[4])
    normed_two, chain_three = tie((normed_two.astype(bf16), chain_three))
    w_shrink = gather_core(chain_three)
    hidden = dot(normed_two, w_expand, (1, 0)) + up_bias
    activated = jax.nn.gelu(hidden, approximate=False).astype(bf16)

    scatter_one = dot(seed, activated, (0, 0)).astype(bf16)
    scatter_one, activated, w_shrink = tie((scatter_one, activated, w_shrink))
    scatter_one = scatter_core(scatter_one)
    branch = dot(activated, w_shrink, (1, 1))
    outputs = give_back(((middle + branch + vectors[5]) * live).astype(bf16))
    grad_hidden = (dot(seed, w_shrink, (1, 0)) * gelu_slope(hidden)).astype(bf16)
    scatter_one, grad_hidden = tie((scatter_one, grad_hidden))
    scatter_one = scatter_ways(scatter_one, 1)
    grad_expand = dot(normed_two, grad_hidden, (0, 0)).astype(bf16)
    grad_normed_two = dot(grad_hidden, w_expand, (1, 1))
    grad_middle = seed_float + backward_norm(grad_normed_two, unit_two, inverse_two, vectors[3])
    grad_attend = grad_middle.astype(bf16)
    scatter_one, grad_attend, grad_expand = tie((scatter_one, grad_attend, grad_expand))
    scatter_one = scatter_ways(scatter_one, 0)
    scatter_two = scatter_core(grad_expand)
    grad_output = dot(grad_attend, mixed, (0, 0)).astype(bf16)
    grad_mixed = dot(grad_attend, w_output, (1, 0)).astype(bf16)
    scatter_one, scatter_two, grad_output, grad_mixed = tie(
        (scatter_one, scatter_two, grad_output, grad_mixed)
    )
    scatter_one = scatter_columns(jnp.concatenate(scatter_one, axis=0), Z_NEAR)
    scatter_two = tuple(
        jnp.concatenate(pair, axis=1) for pair in zip(scatter_core(grad_output), scatter_two)
    )
    grad_mixed, scatter_two = tie((grad_mixed, scatter_two))
    scatter_two = scatter_ways(scatter_two, 1)

    def attend_back(base, grad_mixed):
        return attention_call(
            attend_back_kernel,
            mask,
            [project, grad_mixed],
            n_tp,
            base,
            n_tp // 2,
            3 * width // 2,
            5 * pair_flops // 2,
        )

    early_parts = attend_back(0, grad_mixed)
    early_parts, grad_mixed, scatter_one, scatter_two, outputs = tie(
        (early_parts, grad_mixed, scatter_one, scatter_two, outputs)
    )
    outputs = restored(*outputs)
    scatter_one = scatter_columns(scatter_one, Z_FAR, f32)
    scatter_two = scatter_ways(scatter_two, 0)
    grad_parts = jnp.concatenate([early_parts, attend_back(n_tp // 2, grad_mixed)], axis=1)
    scatter_three = dot(normed_one, grad_parts, (0, 0)).astype(bf16)
    scatter_three, grad_parts, scatter_one = tie((scatter_three, grad_parts, scatter_one))
    grad_shrink = scatter_one.T
    scatter_three = scatter_core(scatter_three)
    grad_normed = dot(grad_parts, w_project, (1, 1))
    scatter_three, grad_normed, scatter_two = tie((scatter_three, grad_normed, scatter_two))
    scatter_three = scatter_ways(scatter_three, 1)
    scatter_two = jnp.concatenate(scatter_two, axis=0)
    scatter_two = [
        scatter_columns(part, Z_NEAR) for part in (scatter_two[:, :width], scatter_two[:, width:])
    ]
    grad_rows = grad_middle + backward_norm(grad_normed, unit_one, inverse_one, vectors[0])
    input_grad = give_back(grad_rows.astype(bf16))
    scatter_three, scatter_two = tie((scatter_three, scatter_two))
    scatter_three = scatter_ways(scatter_three, 0)
    grad_output, grad_expand = (scatter_columns(part, Z_FAR, f32) for part in scatter_two)
    grad_output = grad_output.T
    input_grad, scatter_three = tie((input_grad, scatter_three))
    input_grad = restored(*input_grad)
    scatter_three = scatter_columns(jnp.concatenate(scatter_three, axis=0), Z_NEAR)
    grad_project = scatter_columns(scatter_three, Z_FAR, f32)

    vector_grads = jnp.stack(
        [
            jnp.sum(grad_normed * unit_one, axis=0),
            jnp.sum(grad_normed, axis=0),
            jnp.sum(grad_attend.astype(f32), axis=0),
            jnp.sum(grad_normed_two * unit_two, axis=0),
            jnp.sum(grad_normed_two, axis=0),
            jnp.sum(seed_float, axis=0),
        ]
    )
    vector_grads = lax.dot_general(
        vector_grads,
        placed.astype(f32),
        (((1,), (1,)), ((), ())),
        precision=lax.Precision.HIGHEST,
        preferred_element_type=f32,
    )
    parts_sum = jnp.sum(grad_parts.astype(f32), axis=0).reshape(n_tp, 3, local_width)
    hidden_sum = jnp.sum(grad_hidden.astype(f32), axis=0).reshape(n_tp, ff_local)
    group_grads = jnp.concatenate([parts_sum[:, 0], parts_sum[:, 2], hidden_sum], axis=1)
    wanted = jnp.bitwise_xor(jnp.arange(n_tp, dtype=jnp.int32), z)
    wanted = (wanted % 2) * 2 + wanted // 2
    group_grads = jnp.take(group_grads, wanted, axis=0)
    total = jnp.concatenate([vector_grads.reshape(-1, depth), group_grads.reshape(-1, depth)])
    for step in (CORE, X, Y, Z_NEAR, Z_FAR):
        total = total + swapped(total, *step)
    split = 6 * width // depth
    own_vectors = lax.dynamic_index_in_dim(total[:split].reshape(6, -1, depth), place, 1, False)
    own_groups = lax.dynamic_index_in_dim(total[split:].reshape(n_tp, -1), z, 0, False)
    return (
        outputs,
        input_grad,
        own_vectors[0],
        own_vectors[1],
        grad_project.reshape(depth, 3, local_width),
        own_groups[: 2 * local_width].reshape(2, local_width),
        grad_output,
        own_vectors[2],
        own_vectors[3],
        own_vectors[4],
        grad_expand,
        own_groups[2 * local_width :],
        grad_shrink,
        own_vectors[5],
    )


def solution(mesh):
    one_image_each = mesh.shape["fsdp"] == 8 and mesh.shape["tp"] == 2 * CAP
    return jax.shard_map(
        per_device_whole_image if one_image_each else per_device,
        mesh=mesh,
        in_specs=(
            P("fsdp", "tp", None),
            P("fsdp", "tp", None),
            P("fsdp"),
            P("fsdp"),
            P("fsdp"),
            P("fsdp", None, "tp"),
            P(None, "tp"),
            P("tp", "fsdp"),
            P("fsdp"),
            P("fsdp"),
            P("fsdp"),
            P("fsdp", "tp"),
            P("tp"),
            P("tp", "fsdp"),
            P("fsdp"),
        ),
        out_specs=(
            P("fsdp", "tp", None),
            P("fsdp", "tp", None),
            P("fsdp"),
            P("fsdp"),
            P("fsdp", None, "tp"),
            P(None, "tp"),
            P("tp", "fsdp"),
            P("fsdp"),
            P("fsdp"),
            P("fsdp"),
            P("fsdp", "tp"),
            P("tp"),
            P("tp", "fsdp"),
            P("fsdp"),
        ),
        check_vma=False,
    )
```
